512 devices in a mesh: coil: 16 (over x, z_hi, core), pencil: 32 (over z_lo, y).
Axes of the slice: x: 4, y: 8, z: 8 (z_hi: 2, z_lo: 4; z = z_hi * 4 + z_lo), core: 2. Of those that a mesh axis runs over, the one named last changes fastest.
Arguments:
- kspace: float32 [2, 32, 128, 64, 256], P(None, 'coil', 'pencil'), may hold values from -1.5 to 1.5
- sensitivity: bfloat16 [2, 32, 256, 256, 128], P(None, 'coil', 'pencil'), may hold values from -6 to 6
- line_index: int32 [128, 64], replicated, may hold values from 0 to 255, as said below
Outputs:
- adjoint_image: float32 [2, 256, 256, 128], P(None, 'pencil', 'coil')
The draws below stay inside these ranges and needn't reach their ends.
Inputs may be any that keep to these rules, and one draw needn't show every extreme that they name: `line_index`: in every row, entry j lies in [j * 4, (j + 1) * 4), so a row's lines are distinct and ascending.
All inputs are finite; a program needn't handle non-finite values.
Results may differ from the reference program's by a relative error of at most 0.0003.
Values sent between devices are 32-bit elements; how exact they have to be, the bound alone decides.
A program may use at most 64 MiB of HBM per device.

```python
import jax
import jax.numpy as jnp
from jax import lax

NX = 256
NY = 256
NZ = 128
LINES = 64
COILS = 32


def draw_line_index(key, part):
    key = jax.random.fold_in(key, 11)
    stride = NY // LINES
    jitter = jax.random.randint(key, (NZ, LINES), 0, stride)
    jitter = jitter.at[0, 0].set(0).at[0, LINES - 1].set(stride - 1)
    base = jnp.arange(LINES, dtype=jnp.int32)[None, :] * stride
    return (base + jitter).astype(jnp.int32)


def spiked(array, key, source, target, blocks, factor):
    def block_of(axis_at):
        return (jnp.arange(array.shape[axis_at]) // (array.shape[axis_at] // blocks)).reshape((-1,) + (1,) * (array.ndim - 1 - axis_at))

    near = jax.random.permutation(key, blocks)[block_of(target)]
    second = (block_of(target) + blocks // 2) % blocks
    return jnp.where((block_of(source) == near) | (block_of(source) == second), factor * array, array)


def shard_levels(key, shape, cuts, low, top_value):
    factor_of, own = 1.0, jax.random.fold_in(key, 6)
    for dim, blocks in cuts:
        heights = jnp.exp(jax.random.uniform(jax.random.fold_in(own, dim), (blocks,), jnp.float32, low / len(cuts), top_value / len(cuts)))
        factor_of = factor_of * jnp.repeat(heights, shape[dim] // blocks).reshape([-1 if axis == dim else 1 for axis in range(len(shape))])
    return factor_of


def normal_values(key, extent, deviation, most, pieces=(), kind=jnp.bfloat16):
    result = jax.random.normal(key, extent, jnp.float32) * deviation
    if len(pieces) > 0:
        result = shard_levels(key, extent, pieces, -0.22, 0.18) * result
    return jnp.clip(result, min=-most, max=most).astype(kind)


def bell_draw_with(stream_key, extent, spread, most, cuts, heavy, kind=jnp.bfloat16):
    drawn = spread * jax.random.normal(stream_key, extent, jnp.float32)
    if cuts:
        drawn = drawn * shard_levels(stream_key, extent, cuts, -0.22, 0.18)
    return jnp.clip(spiked(drawn, jax.random.fold_in(stream_key, 3), *heavy), -most, most).astype(kind)


def setup_inputs(seed: int = 0) -> dict:
    seeds = jax.random.split(jax.random.key(seed), 4)
    kspace = normal_values(seeds[0], (2, COILS, NZ, LINES, NX), 0.25, 1.5, ((1, 16), (2, 32)), jnp.float32)
    sensitivity = bell_draw_with(seeds[1], (2, COILS, NX, NY, NZ), 1.0, 6.0, ((1, 16), (2, 32)), (1, 3, 16, 2.0))
    line_index = draw_line_index(jax.random.fold_in(seeds[3], 71), 0)
    return {"kspace": kspace, "sensitivity": sensitivity, "line_index": line_index}


def reference(kspace, sensitivity, line_index):
    scale = 1.0 / (NX * NY * NZ) ** 0.5
    partition = jnp.arange(NZ, dtype=jnp.int32)[:, None]
    coil_first = jnp.transpose(kspace, (1, 0, 2, 3, 4))
    sens_first = jnp.transpose(sensitivity, (1, 0, 2, 3, 4))

    def one_coil(total, inputs):
        spectrum, maps = inputs
        values = spectrum[0] + 1j * spectrum[1]
        grid = jnp.zeros((NZ, NY, NX), values.dtype)
        grid = grid.at[partition, line_index, :].set(values)
        image = jnp.transpose(jnp.fft.ifftn(grid), (2, 1, 0)) * (NX * NY * NZ) * scale
        image_re = jnp.real(image).astype(total.dtype)
        image_im = jnp.imag(image).astype(total.dtype)
        sens_re = maps[0].astype(total.dtype)
        sens_im = maps[1].astype(total.dtype)
        real_part = sens_re * image_re + sens_im * image_im
        imag_part = sens_re * image_im - sens_im * image_re
        return total + jnp.stack([real_part, imag_part]), None

    start = jnp.zeros((2, NX, NY, NZ), jnp.float32)
    total, unused = lax.scan(one_coil, start, (coil_first, sens_first))
    return total
```

```python
import functools
import math

import jax
import jax.numpy as jnp
import ml_dtypes
import numpy as np
from jax import lax
from jax.experimental import pallas as pl
from jax.experimental.pallas import tpu as pltpu
from jax.sharding import PartitionSpec as P

BF16 = jnp.bfloat16
F32 = jnp.float32
MESH = pl.DeviceIdType.MESH
WIDE = 2
NT = (((1,), (1,)), ((), ()))


def two_parts(values):
    high = values.astype(ml_dtypes.bfloat16)
    low = (values - high.astype(np.float64)).astype(ml_dtypes.bfloat16)
    return high, low


def wave(first, second, length):
    angle = (np.outer(first, second) % length) * (2.0 * math.pi / length)
    return np.cos(angle), np.sin(angle)


def readout_table(width, pencils):
    slab = width // pencils
    chunks = slab // WIDE
    cos, sin = wave(np.arange(width), np.arange(width), width)
    rows = np.stack([np.concatenate([cos, -sin], 1), np.concatenate([sin, cos], 1)])
    rows = rows.reshape(2, pencils, chunks, WIDE, 2 * width).transpose(2, 0, 3, 1, 4)
    high, low = two_parts(rows.reshape(chunks, 2 * WIDE * pencils, 2 * width))
    return np.concatenate([high, low, high], 2)


def phase_table(width, lines):
    group = width // lines
    freq = (np.arange(lines)[None, :] * group + np.arange(group)[:, None]).reshape(-1)
    cos, sin = wave(np.arange(width), freq, width)
    rows = np.concatenate([np.concatenate([cos, -sin], 1), np.concatenate([sin, cos], 1)], 0)
    high, low = two_parts(rows)
    return np.concatenate([high, low, high], 1)


def partition_table(width, scale):
    freq = np.arange(width).reshape(width // 2, 2).transpose(1, 0).reshape(-1)
    cos, sin = wave(freq, np.arange(width), width)
    rows = np.concatenate([np.concatenate([cos, sin], 1), np.concatenate([-sin, cos], 1)], 0)
    high, low = two_parts(rows * scale)
    return np.concatenate([high, low, high], 0)


def kernel(
    sizes,
    kspace_hbm,
    sens_hbm,
    lines_ref,
    wx_hbm,
    wy_hbm,
    wz_hbm,
    out_ref,
    kspace,
    sens,
    wx,
    wy,
    wz,
    parts,
    place,
    outbox,
    inbox,
    grid,
    planes,
    mixed,
    share,
    land1,
    land2,
    land3,
    load_sem,
    a_send,
    a_recv,
    s1,
    r1,
    s2,
    r2,
    s3,
    r3,
):
    pencils, coils, chunks, nx, ny, nz, lines = sizes
    ring = coils // 4
    deep = ny // coils
    coil = lax.axis_index("coil")
    me = lax.axis_index("pencil")
    core = coil % 2
    hi = (coil // 2) % 2
    col = coil // 4
    other_core = coil + 1 - 2 * core
    other_hi = coil + 2 - 4 * hi

    loads = [
        pltpu.make_async_copy(src, dst, load_sem.at[i])
        for i, (src, dst) in enumerate(
            [(kspace_hbm, kspace), (wx_hbm, wx), (wy_hbm, wy), (wz_hbm, wz), (sens_hbm, sens)]
        )
    ]
    for load in loads:
        load.start()

    barrier = pltpu.get_barrier_semaphore()

    def greet(to_coil, to_pencil):
        pl.semaphore_signal(
            barrier, inc=1, device_id=(to_coil, to_pencil), device_id_type=MESH
        )

    def greet_pencil(d, carry):
        greet(coil, (me + d) % pencils)
        return carry

    lax.fori_loop(1, pencils, greet_pencil, 0)
    greet(other_core, me)
    greet(other_hi, me)
    for d in range(1, ring):
        greet((coil + 4 * d) % coils, me)

    here = lines_ref[...] - (ny // lines) * lax.broadcasted_iota(jnp.int32, (nz, lines), 1)
    place[...] = jnp.concatenate([here, here], 1)

    loads[0].wait()
    for c in range(2):
        for comp in range(2):
            value = kspace[comp, c]
            high = value.astype(BF16)
            low = (value - high.astype(F32)).astype(BF16)
            parts[c, :, pl.ds(comp * nx, nx)] = high
            parts[c, :, pl.ds((2 + comp) * nx, nx)] = high
            parts[c, :, pl.ds((4 + comp) * nx, nx)] = low
    loads[1].wait()

    def readout(j):
        for c in range(2):
            result = lax.dot_general(wx[j], parts[c], NT, preferred_element_type=F32)
            for q in range(2 * WIDE):
                for zp in range(2):
                    outbox[j, pl.ds(zp * 8 + c * 4 + q, pencils, stride=16), :] = result[
                        q * pencils : (q + 1) * pencils, zp * 128 : (zp + 1) * 128
                    ]

    def a_copy(j, to, size, start):
        return pltpu.make_async_remote_copy(
            src_ref=outbox.at[j, pl.ds(start, size), :],
            dst_ref=inbox.at[j, pl.ds(pl.multiple_of(me * 16, 16) if size == 16 else 0, size), :],
            send_sem=a_send.at[j],
            recv_sem=a_recv.at[j],
            device_id=(coil, to),
            device_id_type=MESH,
        )

    def send(j):
        def one(d, carry):
            to = (me + d) % pencils
            a_copy(j, to, 16, pl.multiple_of(to * 16, 16)).start()
            return carry

        lax.fori_loop(1, pencils, one, 0)
        mine = pl.ds(pl.multiple_of(me * 16, 16), 16)
        inbox[j, mine, :] = outbox[j, mine, :]

    half = lax.broadcasted_iota(jnp.int32, (nz // 2, 128), 1) // 64

    def compute(j):
        for x in range(WIDE):
            for zl in range(2):
                spot = place[pl.ds(zl, nz // 2, stride=2), :]
                keep01 = spot == half
                keep23 = spot == half + 2
                for c in range(2):
                    for comp in range(2):
                        value = inbox[j, pl.ds(c * 4 + comp * 2 + x, nz // 2, stride=8), :]
                        turned = pltpu.roll(value, 64, 1)
                        if zl == 0:
                            both = jnp.where(half == 0, value, turned)
                        else:
                            both = jnp.where(half == 0, turned, value)
                        for k, keep in enumerate((keep01, keep23)):
                            kept = jnp.where(keep, both, 0.0)
                            high = kept.astype(BF16)
                            low = (kept - high.astype(F32)).astype(BF16)
                            rows = pl.ds(c * nz + zl * (nz // 2), nz // 2)
                            at = comp * ny + k * 128
                            grid[x, rows, pl.ds(at, 128)] = high
                            grid[x, rows, pl.ds(2 * ny + at, 128)] = high
                            grid[x, rows, pl.ds(4 * ny + at, 128)] = low
            planes[x] = lax.dot_general(wy[...], grid[x], NT, preferred_element_type=F32)
            for c in range(2):
                for comp in range(2):
                    value = planes[x, pl.ds(comp * ny, ny), pl.ds(c * nz, nz)]
                    high = value.astype(BF16)
                    low = (value - high.astype(F32)).astype(BF16)
                    rows = pl.ds(c * ny, ny)
                    mixed[x, rows, pl.ds(comp * nz, nz)] = high
                    mixed[x, rows, pl.ds((2 + comp) * nz, nz)] = high
                    mixed[x, rows, pl.ds((4 + comp) * nz, nz)] = low
            image = jnp.dot(mixed[x], wz[...], preferred_element_type=F32)
            for slab in range(coils):
                real_part = 0.0
                imag_part = 0.0
                for c in range(2):
                    at = c * ny + slab * deep
                    re = image[at : at + deep, :nz]
                    im = image[at : at + deep, nz:]
                    rows = pl.ds(slab * deep, deep)
                    sre = sens[0, c, j * WIDE + x, rows, :].astype(F32)
                    sim = sens[1, c, j * WIDE + x, rows, :].astype(F32)
                    real_part = real_part + sre * re + sim * im
                    imag_part = imag_part + sre * im - sim * re
                where = (slab % 2, slab // 4, (slab // 2) % 2)
                share[(j,) + where + (0, x)] = real_part
                share[(j,) + where + (1, x)] = imag_part

    def copy1(j):
        return pltpu.make_async_remote_copy(
            src_ref=share.at[j, 1 - core],
            dst_ref=land1.at[j],
            send_sem=s1.at[j],
            recv_sem=r1.at[j],
            device_id=(other_core, me),
            device_id_type=MESH,
        )

    def copy2(j, d):
        return pltpu.make_async_remote_copy(
            src_ref=share.at[j, core, (col + d) % ring],
            dst_ref=land2.at[j, d - 1],
            send_sem=s2.at[j],
            recv_sem=r2.at[j],
            device_id=((coil + 4 * d) % coils, me),
            device_id_type=MESH,
        )

    def all2(j):
        return pltpu.make_async_remote_copy(
            src_ref=land2.at[j],
            dst_ref=land2.at[j],
            send_sem=s2.at[j],
            recv_sem=r2.at[j],
            device_id=((coil + 4) % coils, me),
            device_id_type=MESH,
        )

    def copy3(j):
        return pltpu.make_async_remote_copy(
            src_ref=share.at[j, core, col, 1 - hi],
            dst_ref=land3.at[j],
            send_sem=s3.at[j],
            recv_sem=r3.at[j],
            device_id=(other_hi, me),
            device_id_type=MESH,
        )

    def step2(j):
        copy1(j).wait_recv()
        share[j, core] = share[j, core] + land1[j]
        for d in range(1, ring):
            copy2(j, d).start()

    def step3(j):
        all2(j).wait_recv()
        total = share[j, core, col]
        for d in range(ring - 1):
            total = total + land2[j, d]
        share[j, core, col] = total
        copy3(j).start()

    def step4(j):
        copy3(j).wait_recv()
        total = share[j, core, col, hi] + land3[j]
        for x in range(WIDE):
            for comp in range(2):
                out_ref[comp, j * WIDE + x] = total[comp, x]

    readout(0)
    pl.semaphore_wait(barrier, pencils + ring)
    send(0)

    def early(j, carry):
        readout(j)
        send(j)
        return carry

    lax.fori_loop(1, chunks, early, 0)
    for load in loads[2:]:
        load.wait()

    def turn(j, carry):
        a_copy(j, me, (pencils - 1) * 16, 0).wait_recv()
        compute(j)
        copy1(j).start()

        @pl.when(j >= 1)
        def _():
            step3(j - 1)

        step2(j)

        @pl.when(j >= 2)
        def _():
            step4(j - 2)

        return carry

    lax.fori_loop(0, chunks, turn, 0)
    step4(chunks - 2)
    step3(chunks - 1)

    def drain(j, carry):
        a_copy(j, me, (pencils - 1) * 16, 0).wait_send()
        copy1(j).wait_send()
        all2(j).wait_send()
        copy3(j).wait_send()
        return carry

    lax.fori_loop(0, chunks, drain, 0)
    step4(chunks - 1)


def on_device(coils, pencils, kspace, sensitivity, line_index):
    _, coil_dev, part_dev, lines, nx = kspace.shape
    slab, ny, nz = sensitivity.shape[2:]
    chunks = slab // WIDE
    ring = coils // 4
    deep = ny // coils
    sizes = (pencils, coils, chunks, nx, ny, nz, lines)
    scale = 1.0 / math.sqrt(nx * ny * nz)
    rows = part_dev * lines
    wx = jnp.asarray(readout_table(nx, pencils))
    wy = jnp.asarray(phase_table(ny, lines))
    wz = jnp.asarray(partition_table(nz, scale))
    block = (2, WIDE, deep, nz)
    vmem = pltpu.VMEM
    dma = pltpu.SemaphoreType.DMA
    flat = kspace.reshape(2, coil_dev, rows, nx)
    return pl.pallas_call(
        functools.partial(kernel, sizes),
        out_shape=jax.ShapeDtypeStruct((2, slab, deep, nz), F32),
        in_specs=[
            pl.BlockSpec(memory_space=pl.ANY),
            pl.BlockSpec(memory_space=pl.ANY),
            pl.BlockSpec(memory_space=pltpu.VMEM),
            pl.BlockSpec(memory_space=pl.ANY),
            pl.BlockSpec(memory_space=pl.ANY),
            pl.BlockSpec(memory_space=pl.ANY),
        ],
        out_specs=pl.BlockSpec(memory_space=pltpu.VMEM),
        scratch_shapes=[
            vmem(flat.shape, F32),
            vmem(sensitivity.shape, BF16),
            vmem(wx.shape, BF16),
            vmem(wy.shape, BF16),
            vmem(wz.shape, BF16),
            vmem((coil_dev, rows, 6 * nx), BF16),
            vmem((nz, 2 * lines), jnp.int32),
            vmem((chunks, pencils * 16, 128), F32),
            vmem((chunks, pencils * 16, 128), F32),
            vmem((WIDE, coil_dev * nz, 6 * ny), BF16),
            vmem((WIDE, 2 * ny, coil_dev * nz), F32),
            vmem((WIDE, coil_dev * ny, 6 * nz), BF16),
            vmem((chunks, 2, ring, 2) + block, F32),
            vmem((chunks, ring, 2) + block, F32),
            vmem((chunks, ring - 1, 2) + block, F32),
            vmem((chunks,) + block, F32),
            dma((5,)),
        ]
        + [dma((chunks,)) for _ in range(8)],
        compiler_params=pltpu.CompilerParams(
            collective_id=0, has_side_effects=True, vmem_limit_bytes=48 * 1024 * 1024
        ),
    )(flat, sensitivity, line_index, wx, wy, wz)


def solution(mesh):
    in_specs = (P(None, "coil", "pencil", None, None), P(None, "coil", "pencil", None, None), P())
    out_specs = P(None, "pencil", "coil", None)
    return jax.shard_map(
        functools.partial(on_device, mesh.shape["coil"], mesh.shape["pencil"]),
        mesh=mesh,
        in_specs=in_specs,
        out_specs=out_specs,
        check_vma=False,
    )
```

```python
import functools
import math

import jax
import jax.numpy as jnp
import ml_dtypes
import numpy as np
from jax import lax
from jax.experimental import pallas as pl
from jax.experimental.pallas import tpu as pltpu
from jax.sharding import PartitionSpec as P

BF16 = jnp.bfloat16
F32 = jnp.float32
MESH = pl.DeviceIdType.MESH
WIDE = 2
RING_Y = 8
BLOCK = 8
NT = (((1,), (1,)), ((), ()))


def two_parts(values):
    high = values.astype(ml_dtypes.bfloat16)
    low = (values - high.astype(np.float64)).astype(ml_dtypes.bfloat16)
    return high, low


def wave(first, second, length):
    angle = (np.outer(first, second) % length) * (2.0 * math.pi / length)
    return np.cos(angle), np.sin(angle)


def readout_table(width, pencils):
    slab = width // pencils
    chunks = slab // WIDE
    cos, sin = wave(np.arange(width), np.arange(width), width)
    rows = np.stack([np.concatenate([cos, -sin], 1), np.concatenate([sin, cos], 1)])
    rows = rows.reshape(2, pencils, chunks, WIDE, 2 * width).transpose(2, 3, 0, 1, 4)
    high, low = two_parts(rows.reshape(chunks, 2 * WIDE * pencils, 2 * width))
    return np.concatenate([high, low, high], 2)


def phase_table(width, lines, slabs):
    group = width // lines
    freq = (np.arange(lines)[None, :] * group + np.arange(group)[:, None]).reshape(-1)
    cos, sin = wave(np.arange(width), freq, width)
    rows = np.stack([np.concatenate([cos, -sin], 1), np.concatenate([sin, cos], 1)])
    rows = rows.reshape(2, slabs // 2, 2, width // slabs, 2 * width).transpose(2, 0, 1, 3, 4)
    high, low = two_parts(rows.reshape(2, width, 2 * width))
    return np.concatenate([high, low, high], 2)


def partition_table(width, scale):
    freq = np.arange(width).reshape(width // 2, 2).transpose(1, 0).reshape(-1)
    cos, sin = wave(freq, np.arange(width), width)
    rows = np.concatenate([np.concatenate([cos, sin], 1), np.concatenate([-sin, cos], 1)], 0)
    high, low = two_parts(rows * scale)
    return np.concatenate([high, low, high], 0)


def kernel(
    sizes,
    kspace_hbm,
    sens_hbm,
    lines_ref,
    wx_hbm,
    wy_hbm,
    wz_hbm,
    out_ref,
    kspace,
    sens,
    wx,
    wy,
    wz,
    parts,
    place,
    outbox,
    inbox,
    grid,
    planes,
    mixed,
    share,
    land1,
    land2,
    land3,
    land4,
    load_sem,
    a_send,
    a_recv,
    s1,
    r1,
    s2,
    r2,
    s3,
    r3,
    s4,
):
    pencils, coils, chunks, nx, ny, nz, lines = sizes
    ring = coils // 4
    deep = ny // coils
    coil = lax.axis_index("coil")
    me = lax.axis_index("pencil")
    core = coil % 2
    hi = coil // 2 % 2
    col = coil // 4
    other_core = coil + 1 - 2 * core
    other_hi = coil + 2 - 4 * hi

    loads = [
        pltpu.make_async_copy(src, dst, load_sem.at[i])
        for i, (src, dst) in enumerate(
            [(kspace_hbm, kspace), (wx_hbm, wx), (wy_hbm, wy), (wz_hbm, wz), (sens_hbm, sens)]
        )
    ]
    for load in loads[:2]:
        load.start()

    barrier = pltpu.get_barrier_semaphore()

    def greet(to_coil, to_pencil):
        pl.semaphore_signal(
            barrier, inc=1, device_id=(to_coil, to_pencil), device_id_type=MESH
        )

    def greet_pencil(d, carry):
        greet(coil, (me + d) % pencils)
        return carry

    lax.fori_loop(1, pencils, greet_pencil, 0)
    greet(other_core, me)
    for d in range(1, coils // 2):
        greet((coil + 2 * d) % coils, me)

    here = lines_ref[...] - (ny // lines) * lax.broadcasted_iota(jnp.int32, (lines, nz), 0)
    place[...] = jnp.concatenate([here, here], 0).T

    loads[0].wait()
    for load in loads[2:]:
        load.start()
    for c in range(2):
        for comp in range(2):
            value = kspace[comp, c]
            high = value.astype(BF16)
            low = (value - high.astype(F32)).astype(BF16)
            parts[c, :, pl.ds(comp * nx, nx)] = high
            parts[c, :, pl.ds((2 + comp) * nx, nx)] = high
            parts[c, :, pl.ds((4 + comp) * nx, nx)] = low
    loads[1].wait()

    def readout(j):
        for c in range(2):
            result = lax.dot_general(wx[j], parts[c], NT, preferred_element_type=F32)
            for x in range(WIDE):
                for comp in range(2):
                    rows = (x * 2 + comp) * pencils
                    for zp in range(2):
                        to = pl.ds(zp * 4 + c * 2 + comp, pencils, stride=BLOCK)
                        outbox[j * WIDE + x, to, :] = result[
                            rows : rows + pencils, zp * 128 : (zp + 1) * 128
                        ]

    def at(pencil):
        return pl.ds(pl.multiple_of(pencil * BLOCK, BLOCK), BLOCK)

    def a_copy(x, count, to):
        return pltpu.make_async_remote_copy(
            src_ref=outbox.at[pl.ds(x, count), at(to), :],
            dst_ref=inbox.at[pl.ds(x, count), at(me), :],
            send_sem=a_send.at[x],
            recv_sem=a_recv.at[x],
            device_id=(coil, to),
            device_id_type=MESH,
        )

    def a_many(x, count):
        return pltpu.make_async_remote_copy(
            src_ref=outbox.at[pl.ds(x, count), pl.ds(0, (pencils - 1) * BLOCK), :],
            dst_ref=inbox.at[pl.ds(x, count), pl.ds(0, (pencils - 1) * BLOCK), :],
            send_sem=a_send.at[x],
            recv_sem=a_recv.at[x],
            device_id=(coil, me),
            device_id_type=MESH,
        )

    def send(x, count):
        def one(i, carry):
            k, g = i // RING_Y, i % RING_Y
            dy = 1 + g // 4 + 4 * (g % 2) + 2 * (g % 4 // 2)
            dz = k + g + 2
            to = (me // RING_Y + dz) % (pencils // RING_Y) * RING_Y + (me + dy) % RING_Y
            a_copy(x, count, to).start()
            return carry

        lax.fori_loop(0, pencils - 1, one, 0)
        for k in range(count):
            inbox[x + k, at(me), :] = outbox[x + k, at(me), :]

    half = lax.broadcasted_iota(jnp.int32, (nz // 2, 128), 1) // 64

    def fill(x, buf):
        for zl in range(2):
            spot = place[pl.ds(zl, nz // 2, stride=2), :]
            keep01 = spot == half
            keep23 = spot == half + 2
            for c in range(2):
                for comp in range(2):
                    value = inbox[x, pl.ds(c * 2 + comp, nz // 2, stride=4), :]
                    turned = pltpu.roll(value, 64, 1)
                    if zl == 0:
                        both = jnp.where(half == 0, value, turned)
                    else:
                        both = jnp.where(half == 0, turned, value)
                    for k, keep in enumerate((keep01, keep23)):
                        kept = jnp.where(keep, both, 0.0)
                        high = kept.astype(BF16)
                        low = (kept - high.astype(F32)).astype(BF16)
                        rows = pl.ds(c * nz + zl * (nz // 2), nz // 2)
                        left = comp * ny + k * 128
                        grid[buf, rows, pl.ds(left, 128)] = high
                        grid[buf, rows, pl.ds(2 * ny + left, 128)] = high
                        grid[buf, rows, pl.ds(4 * ny + left, 128)] = low

    def combine(x, buf):
        tall = ny // 2
        table = wy[...].reshape(2 * ny, 6 * ny)
        planes[...] = lax.dot_general(table, grid[buf], NT, preferred_element_type=F32)
        for part in range(2):
            for c in range(2):
                for comp in range(2):
                    value = planes[pl.ds(part * ny + comp * tall, tall), pl.ds(c * nz, nz)]
                    high = value.astype(BF16)
                    low = (value - high.astype(F32)).astype(BF16)
                    rows = pl.ds(part * ny + c * tall, tall)
                    mixed[rows, pl.ds(comp * nz, nz)] = high
                    mixed[rows, pl.ds((2 + comp) * nz, nz)] = high
                    mixed[rows, pl.ds((4 + comp) * nz, nz)] = low
        image = jnp.dot(mixed[...], wz[...], preferred_element_type=F32)
        for part in range(2):
            for m in range(coils // 2):
                real_part = 0.0
                imag_part = 0.0
                for c in range(2):
                    top = part * ny + c * tall + m * deep
                    re = image[top : top + deep, :nz]
                    im = image[top : top + deep, nz:]
                    rows = pl.ds((2 * m + part) * deep, deep)
                    sre = sens[0, c, x, rows, :].astype(F32)
                    sim = sens[1, c, x, rows, :].astype(F32)
                    real_part = real_part + sre * re + sim * im
                    imag_part = imag_part + sre * im - sim * re
                share[x, part, m // 2, m % 2, 0] = real_part
                share[x, part, m // 2, m % 2, 1] = imag_part

    def compute(x, buf):
        fill(x, buf)
        combine(x, buf)
        copy1(x).start()

    def copy1(j):
        return pltpu.make_async_remote_copy(
            src_ref=share.at[j, 1 - core],
            dst_ref=land1.at[j],
            send_sem=s1.at[j],
            recv_sem=r1.at[j],
            device_id=(other_core, me),
            device_id_type=MESH,
        )

    def copy2(j, d):
        return pltpu.make_async_remote_copy(
            src_ref=share.at[j, core, (col + d) % ring],
            dst_ref=land2.at[j, d - 1],
            send_sem=s2.at[j],
            recv_sem=r2.at[j],
            device_id=((coil + 4 * d) % coils, me),
            device_id_type=MESH,
        )

    def all2(j):
        return pltpu.make_async_remote_copy(
            src_ref=land2.at[j],
            dst_ref=land2.at[j],
            send_sem=s2.at[j],
            recv_sem=r2.at[j],
            device_id=((coil + 4) % coils, me),
            device_id_type=MESH,
        )

    def copy3(j):
        return pltpu.make_async_remote_copy(
            src_ref=share.at[j, core, col, 1 - hi],
            dst_ref=land3.at[j],
            send_sem=s3.at[j],
            recv_sem=r3.at[j],
            device_id=(other_hi, me),
            device_id_type=MESH,
        )

    def straight(d):
        to = (coil + 2 * d) % coils
        return pltpu.make_async_remote_copy(
            src_ref=share.at[final, core, to // 4, to // 2 % 2],
            dst_ref=land4.at[d - 1],
            send_sem=s4.at[0],
            recv_sem=s4.at[1],
            device_id=(to, me),
            device_id_type=MESH,
        )

    def all4():
        return pltpu.make_async_remote_copy(
            src_ref=land4,
            dst_ref=land4,
            send_sem=s4.at[0],
            recv_sem=s4.at[1],
            device_id=(other_hi, me),
            device_id_type=MESH,
        )

    def step2(x):
        copy1(x).wait_recv()
        share[x, core] = share[x, core] + land1[x]

        def usual():
            for d in range(1, ring):
                copy2(x, d).start()

        def direct():
            for d in range(1, coils // 2):
                straight(d).start()

        if isinstance(x, int) and x == final:
            direct()
        else:
            usual()

    def sum3(x):
        all2(x).wait_recv()
        total = share[x, core, col]
        for d in range(ring - 1):
            total = total + land2[x, d]
        share[x, core, col] = total

    def send3(x):
        copy3(x).start()

    def finish(x):
        copy3(x).wait_recv()
        total = share[x, core, col, hi] + land3[x]
        for comp in range(2):
            out_ref[comp, x] = total[comp]

    def finish_last():
        all4().wait_recv()
        total = share[final, core, col, hi]
        for d in range(coils // 2 - 1):
            total = total + land4[d]
        for comp in range(2):
            out_ref[comp, final] = total[comp]

    last = chunks - 1
    final = chunks * WIDE - 1

    def early(j):
        readout(j)

        @pl.when(j < last)
        def _():
            send(j * WIDE, 2)

        @pl.when(j == last)
        def _():
            send(j * WIDE, 1)
            send(j * WIDE + 1, 1)

    readout(0)
    pl.semaphore_wait(barrier, pencils - 1 + coils // 2)
    send(0, 2)
    readout(1)
    send(2, 2)
    for load in loads[2:]:
        load.wait()

    def turn(j, carry):
        x = j * WIDE

        @pl.when(j + 2 <= last)
        def _():
            early(j + 2)

        @pl.when(j < last)
        def _():
            a_many(x, 2).wait_recv()

        @pl.when(j == last)
        def _():
            a_many(x, 1).wait_recv()

        compute(x, 0)

        @pl.when(j >= 1)
        def _():
            step2(x - 1)

        @pl.when(j == last)
        def _():
            for k in (3, 2):
                sum3(x - k)
                send3(x - k)
            a_many(x + 1, 1).wait_recv()

        compute(x + 1, 1)
        step2(x)

        @pl.when((j >= 2) & (j < last))
        def _():
            sum3(x - 3)
            send3(x - 3)

        @pl.when((j >= 1) & (j < last))
        def _():
            sum3(x - 2)
            send3(x - 2)

        return carry

    lax.fori_loop(0, chunks, turn, 0)
    x = last * WIDE
    for k in range(x - 3):
        finish(k)
    step2(final)
    for k in (x - 1, x):
        sum3(k)
        send3(k)
    for k in range(x - 3, x):
        finish(k)

    def drain(j, carry):
        copy1(j).wait_send()
        all2(j).wait_send()
        copy3(j).wait_send()
        return carry

    for j in range(last):
        a_many(j * WIDE, 2).wait_send()
    a_many(x, 1).wait_send()
    a_many(x + 1, 1).wait_send()
    lax.fori_loop(0, x, drain, 0)
    finish(x)
    finish_last()
    drain(x, 0)
    copy1(final).wait_send()
    all4().wait_send()


def on_device(coils, pencils, kspace, sensitivity, line_index):
    _, coil_dev, part_dev, lines, nx = kspace.shape
    slab, ny, nz = sensitivity.shape[2:]
    chunks = slab // WIDE
    ring = coils // 4
    deep = ny // coils
    sizes = (pencils, coils, chunks, nx, ny, nz, lines)
    scale = 1.0 / math.sqrt(nx * ny * nz)
    rows = part_dev * lines
    wx = jnp.asarray(readout_table(nx, pencils))
    wy = jnp.asarray(phase_table(ny, lines, coils))
    wz = jnp.asarray(partition_table(nz, scale))
    block = (2, deep, nz)
    vmem = pltpu.VMEM
    dma = pltpu.SemaphoreType.DMA
    flat = kspace.reshape(2, coil_dev, rows, nx)
    return pl.pallas_call(
        functools.partial(kernel, sizes),
        out_shape=jax.ShapeDtypeStruct((2, slab, deep, nz), F32),
        in_specs=[
            pl.BlockSpec(memory_space=pl.ANY),
            pl.BlockSpec(memory_space=pl.ANY),
            pl.BlockSpec(memory_space=pltpu.VMEM),
            pl.BlockSpec(memory_space=pl.ANY),
            pl.BlockSpec(memory_space=pl.ANY),
            pl.BlockSpec(memory_space=pl.ANY),
        ],
        out_specs=pl.BlockSpec(memory_space=pltpu.VMEM),
        scratch_shapes=[
            vmem(flat.shape, F32),
            vmem(sensitivity.shape, BF16),
            vmem(wx.shape, BF16),
            vmem(wy.shape, BF16),
            vmem(wz.shape, BF16),
            vmem((coil_dev, rows, 6 * nx), BF16),
            vmem((nz, 2 * lines), jnp.int32),
            vmem((slab, pencils * BLOCK, 128), F32),
            vmem((slab, pencils * BLOCK, 128), F32),
            vmem((WIDE, coil_dev * nz, 6 * ny), BF16),
            vmem((2 * ny, coil_dev * nz), F32),
            vmem((2 * ny, 6 * nz), BF16),
            vmem((slab, 2, ring, 2) + block, F32),
            vmem((slab, ring, 2) + block, F32),
            vmem((slab, ring - 1, 2) + block, F32),
            vmem((slab,) + block, F32),
            vmem((coils // 2 - 1,) + block, F32),
            dma((5,)),
        ]
        + [dma((slab,)) for _ in range(8)]
        + [dma((2,))],
        compiler_params=pltpu.CompilerParams(
            collective_id=0, has_side_effects=True, vmem_limit_bytes=62 * 1024 * 1024
        ),
    )(flat, sensitivity, line_index.T, wx, wy, wz)


def solution(mesh):
    in_specs = (P(None, "coil", "pencil", None, None), P(None, "coil", "pencil", None, None), P())
    out_specs = P(None, "pencil", "coil", None)
    return jax.shard_map(
        functools.partial(on_device, mesh.shape["coil"], mesh.shape["pencil"]),
        mesh=mesh,
        in_specs=in_specs,
        out_specs=out_specs,
        check_vma=False,
    )
```

```python
import functools
import math

import jax
import jax.numpy as jnp
import ml_dtypes
import numpy as np
from jax import lax
from jax.experimental import pallas as pl
from jax.experimental.pallas import tpu as pltpu
from jax.sharding import PartitionSpec as P

BF16 = jnp.bfloat16
F32 = jnp.float32
MESH = pl.DeviceIdType.MESH
WIDE = 2
RING_Y = 8
BLOCK = 8
NT = (((1,), (1,)), ((), ()))


def two_parts(values):
    high = values.astype(ml_dtypes.bfloat16)
    low = (values - high.astype(np.float64)).astype(ml_dtypes.bfloat16)
    return high, low


def wave(first, second, length):
    angle = (np.outer(first, second) % length) * (2.0 * math.pi / length)
    return np.cos(angle), np.sin(angle)


def readout_table(width, pencils):
    slab = width // pencils
    chunks = slab // WIDE
    cos, sin = wave(np.arange(width), np.arange(width), width)
    rows = np.stack([np.concatenate([cos, -sin], 1), np.concatenate([sin, cos], 1)])
    rows = rows.reshape(2, pencils, chunks, WIDE, 2 * width).transpose(2, 3, 0, 1, 4)
    high, low = two_parts(rows.reshape(chunks, 2 * WIDE * pencils, 2 * width))
    return np.concatenate([high, low, high], 2)


def phase_table(width, lines, slabs):
    group = width // lines
    freq = (np.arange(lines)[None, :] * group + np.arange(group)[:, None]).reshape(-1)
    cos, sin = wave(np.arange(width), freq, width)
    rows = np.stack([np.concatenate([cos, -sin], 1), np.concatenate([sin, cos], 1)])
    rows = rows.reshape(2, slabs // 2, 2, width // slabs, 2 * width).transpose(2, 0, 1, 3, 4)
    high, low = two_parts(rows.reshape(2, width, 2 * width))
    return np.concatenate([high, low, high], 2)


def partition_table(width, scale):
    freq = np.arange(width).reshape(width // 2, 2).transpose(1, 0).reshape(-1)
    cos, sin = wave(freq, np.arange(width), width)
    rows = np.concatenate([np.concatenate([cos, sin], 1), np.concatenate([-sin, cos], 1)], 0)
    high, low = two_parts(rows * scale)
    return np.concatenate([high, low, high], 0)


def kernel(
    sizes,
    kspace_hbm,
    sens_hbm,
    lines_hbm,
    wx_hbm,
    wy_hbm,
    wz_hbm,
    out_ref,
    kspace,
    sens,
    lines_ref,
    wx,
    wy,
    wz,
    parts,
    place,
    outbox,
    inbox,
    grid,
    planes,
    mixed,
    share,
    land1,
    land2,
    land3,
    land4,
    load_sem,
    a_send,
    a_recv,
    s1,
    r1,
    s2,
    r2,
    s3,
    r3,
    s4,
):
    pencils, coils, chunks, nx, ny, nz, lines = sizes
    ring = coils // 4
    deep = ny // coils
    coil = lax.axis_index("coil")
    me = lax.axis_index("pencil")
    core = coil % 2
    hi = coil // 2 % 2
    col = coil // 4
    other_core = coil + 1 - 2 * core
    other_hi = coil + 2 - 4 * hi

    pairs = [
        (kspace_hbm, kspace),
        (wx_hbm.at[0], wx.at[0]),
        (wx_hbm.at[pl.ds(1, chunks - 1)], wx.at[pl.ds(1, chunks - 1)]),
        (lines_hbm, lines_ref),
        (wy_hbm, wy),
        (wz_hbm, wz),
        (sens_hbm, sens),
    ]
    loads = [
        pltpu.make_async_copy(src, dst, load_sem.at[i]) for i, (src, dst) in enumerate(pairs)
    ]
    for load in loads[:2]:
        load.start()

    barrier = pltpu.get_barrier_semaphore()

    def greet(to_coil, to_pencil):
        pl.semaphore_signal(
            barrier, inc=1, device_id=(to_coil, to_pencil), device_id_type=MESH
        )

    def greet_pencil(d, carry):
        greet(coil, (me + d) % pencils)
        return carry

    lax.fori_loop(1, pencils, greet_pencil, 0)
    greet(other_core, me)
    for d in range(1, coils // 2):
        greet((coil + 2 * d) % coils, me)

    loads[0].wait()
    for load in loads[2:]:
        load.start()
    for c in range(2):
        for comp in range(2):
            value = kspace[comp, c]
            high = value.astype(BF16)
            low = (value - high.astype(F32)).astype(BF16)
            parts[c, :, pl.ds(comp * nx, nx)] = high
            parts[c, :, pl.ds((2 + comp) * nx, nx)] = high
            parts[c, :, pl.ds((4 + comp) * nx, nx)] = low
    loads[1].wait()

    def readout(j):
        for c in range(2):
            result = lax.dot_general(wx[j], parts[c], NT, preferred_element_type=F32)
            for x in range(WIDE):
                for comp in range(2):
                    rows = (x * 2 + comp) * pencils
                    for zp in range(2):
                        to = pl.ds(zp * 4 + c * 2 + comp, pencils, stride=BLOCK)
                        outbox[j * WIDE + x, to, :] = result[
                            rows : rows + pencils, zp * 128 : (zp + 1) * 128
                        ]

    def at(pencil):
        return pl.ds(pl.multiple_of(pencil * BLOCK, BLOCK), BLOCK)

    def a_copy(x, count, to):
        return pltpu.make_async_remote_copy(
            src_ref=outbox.at[pl.ds(x, count), at(to), :],
            dst_ref=inbox.at[pl.ds(x, count), at(me), :],
            send_sem=a_send.at[x],
            recv_sem=a_recv.at[x],
            device_id=(coil, to),
            device_id_type=MESH,
        )

    def a_many(x, count):
        return pltpu.make_async_remote_copy(
            src_ref=outbox.at[pl.ds(x, count), pl.ds(0, (pencils - 1) * BLOCK), :],
            dst_ref=inbox.at[pl.ds(x, count), pl.ds(0, (pencils - 1) * BLOCK), :],
            send_sem=a_send.at[x],
            recv_sem=a_recv.at[x],
            device_id=(coil, me),
            device_id_type=MESH,
        )

    def send(x, count):
        def one(i, carry):
            k, g = i // RING_Y, i % RING_Y
            dy = 1 + g // 4 + 4 * (g % 2) + 2 * (g % 4 // 2)
            dz = k + g + 2
            to = (me // RING_Y + dz) % (pencils // RING_Y) * RING_Y + (me + dy) % RING_Y
            a_copy(x, count, to).start()
            return carry

        lax.fori_loop(0, pencils - 1, one, 0)
        for k in range(count):
            inbox[x + k, at(me), :] = outbox[x + k, at(me), :]

    half = lax.broadcasted_iota(jnp.int32, (nz // 2, 128), 1) // 64

    def fill(x, buf):
        for zl in range(2):
            spot = place[pl.ds(zl, nz // 2, stride=2), :]
            keep01 = spot == half
            keep23 = spot == half + 2
            for c in range(2):
                for comp in range(2):
                    value = inbox[x, pl.ds(c * 2 + comp, nz // 2, stride=4), :]
                    turned = pltpu.roll(value, 64, 1)
                    if zl == 0:
                        both = jnp.where(half == 0, value, turned)
                    else:
                        both = jnp.where(half == 0, turned, value)
                    for k, keep in enumerate((keep01, keep23)):
                        kept = jnp.where(keep, both, 0.0)
                        high = kept.astype(BF16)
                        low = (kept - high.astype(F32)).astype(BF16)
                        rows = pl.ds(c * nz + zl * (nz // 2), nz // 2)
                        left = comp * ny + k * 128
                        grid[buf, rows, pl.ds(left, 128)] = high
                        grid[buf, rows, pl.ds(2 * ny + left, 128)] = high
                        grid[buf, rows, pl.ds(4 * ny + left, 128)] = low

    def transform(buf, part, count):
        tall = ny // 2
        top = part if count == 1 else 0
        table = wy[pl.ds(top, count)].reshape(count * ny, 6 * ny)
        planes[pl.ds(0, count * ny), :] = lax.dot_general(
            table, grid[buf], NT, preferred_element_type=F32
        )
        for p in range(count):
            for c in range(2):
                for comp in range(2):
                    value = planes[pl.ds(p * ny + comp * tall, tall), pl.ds(c * nz, nz)]
                    high = value.astype(BF16)
                    low = (value - high.astype(F32)).astype(BF16)
                    rows = pl.ds(p * ny + c * tall, tall)
                    mixed[rows, pl.ds(comp * nz, nz)] = high
                    mixed[rows, pl.ds((2 + comp) * nz, nz)] = high
                    mixed[rows, pl.ds((4 + comp) * nz, nz)] = low
        return jnp.dot(mixed[pl.ds(0, count * ny), :], wz[...], preferred_element_type=F32)

    def combine(x, buf, part, count):
        image = transform(buf, part, count)
        for p in range(count):
            home = part if count == 1 else p
            for m in range(coils // 2):
                real_part = 0.0
                imag_part = 0.0
                for c in range(2):
                    top = p * ny + c * (ny // 2) + m * deep
                    re = image[top : top + deep, :nz]
                    im = image[top : top + deep, nz:]
                    first = (2 * m + home) * deep
                    if count == 1:
                        first = pl.multiple_of(first, deep)
                    sre = sens[0, c, x, pl.ds(first, deep), :].astype(F32)
                    sim = sens[1, c, x, pl.ds(first, deep), :].astype(F32)
                    real_part = real_part + sre * re + sim * im
                    imag_part = imag_part + sre * im - sim * re
                share[x, home, m // 2, m % 2, 0] = real_part
                share[x, home, m // 2, m % 2, 1] = imag_part

    def compute(x, buf):
        fill(x, buf)
        combine(x, buf, 0, 2)
        copy1(x).start()

    def compute_halves(x, buf):
        fill(x, buf)
        combine(x, buf, 1 - core, 1)
        copy1(x).start()
        combine(x, buf, core, 1)

    def copy1(j):
        return pltpu.make_async_remote_copy(
            src_ref=share.at[j, 1 - core],
            dst_ref=land1.at[j],
            send_sem=s1.at[j],
            recv_sem=r1.at[j],
            device_id=(other_core, me),
            device_id_type=MESH,
        )

    def copy2(j, d):
        return pltpu.make_async_remote_copy(
            src_ref=share.at[j, core, (col + d) % ring],
            dst_ref=land2.at[j, d - 1],
            send_sem=s2.at[j],
            recv_sem=r2.at[j],
            device_id=((coil + 4 * d) % coils, me),
            device_id_type=MESH,
        )

    def all2(j):
        return pltpu.make_async_remote_copy(
            src_ref=land2.at[j],
            dst_ref=land2.at[j],
            send_sem=s2.at[j],
            recv_sem=r2.at[j],
            device_id=((coil + 4) % coils, me),
            device_id_type=MESH,
        )

    def copy3(j):
        return pltpu.make_async_remote_copy(
            src_ref=share.at[j, core, col, 1 - hi],
            dst_ref=land3.at[j],
            send_sem=s3.at[j],
            recv_sem=r3.at[j],
            device_id=(other_hi, me),
            device_id_type=MESH,
        )

    def straight(d):
        to = (coil + 2 * d) % coils
        return pltpu.make_async_remote_copy(
            src_ref=share.at[final, core, to // 4, to // 2 % 2],
            dst_ref=land4.at[d - 1],
            send_sem=s4.at[0],
            recv_sem=s4.at[1],
            device_id=(to, me),
            device_id_type=MESH,
        )

    def all4():
        return pltpu.make_async_remote_copy(
            src_ref=land4,
            dst_ref=land4,
            send_sem=s4.at[0],
            recv_sem=s4.at[1],
            device_id=(other_hi, me),
            device_id_type=MESH,
        )

    def step2(x):
        copy1(x).wait_recv()
        share[x, core] = share[x, core] + land1[x]

        def usual():
            for d in range(1, ring):
                copy2(x, d).start()

        def direct():
            for d in range(1, coils // 2):
                straight(d).start()

        if isinstance(x, int) and x == final:
            direct()
        else:
            usual()

    def sum3(x):
        all2(x).wait_recv()
        total = share[x, core, col]
        for d in range(ring - 1):
            total = total + land2[x, d]
        share[x, core, col] = total

    def send3(x):
        copy3(x).start()

    def finish(x):
        copy3(x).wait_recv()
        total = share[x, core, col, hi] + land3[x]
        for comp in range(2):
            out_ref[comp, x] = total[comp]

    def finish_last():
        all4().wait_recv()
        total = share[final, core, col, hi]
        for d in range(coils // 2 - 1):
            total = total + land4[d]
        for comp in range(2):
            out_ref[comp, final] = total[comp]

    last = chunks - 1
    final = chunks * WIDE - 1

    def early(j):
        readout(j)

        @pl.when(j < last)
        def _():
            send(j * WIDE, 2)

        @pl.when(j == last)
        def _():
            send(j * WIDE, 1)
            send(j * WIDE + 1, 1)

    readout(0)
    pl.semaphore_wait(barrier, pencils - 1 + coils // 2)
    send(0, 2)
    loads[2].wait()
    readout(1)
    send(2, 2)
    loads[3].wait()
    here = lines_ref[...] - (ny // lines) * lax.broadcasted_iota(jnp.int32, (lines, nz), 0)
    place[...] = jnp.concatenate([here, here], 0).T

    for load in loads[4:]:
        load.wait()

    def turn(j, carry):
        x = j * WIDE

        @pl.when(j + 2 <= last)
        def _():
            early(j + 2)

        a_many(x, 2).wait_recv()
        fill(x, 0)
        fill(x + 1, 1)
        combine(x, 0, 0, 2)
        copy1(x).start()

        @pl.when(j >= 1)
        def _():
            step2(x - 1)

        combine(x + 1, 1, 0, 2)
        copy1(x + 1).start()
        step2(x)

        @pl.when(j >= 2)
        def _():
            sum3(x - 3)
            send3(x - 3)

        @pl.when(j >= 1)
        def _():
            sum3(x - 2)
            send3(x - 2)

        return carry

    lax.fori_loop(0, last, turn, 0)
    x = last * WIDE
    a_many(x, 1).wait_recv()
    compute(x, 0)
    step2(x - 1)
    for k in (3, 2):
        sum3(x - k)
        send3(x - k)
    a_many(x + 1, 1).wait_recv()
    step2(x)
    compute_halves(final, 1)
    sum3(x - 1)
    send3(x - 1)
    step2(final)
    for k in range(x - 3):
        finish(k)
    sum3(x)
    send3(x)
    for k in range(x - 3, x):
        finish(k)

    def drain(j, carry):
        copy1(j).wait_send()
        all2(j).wait_send()
        copy3(j).wait_send()
        return carry

    for j in range(last):
        a_many(j * WIDE, 2).wait_send()
    a_many(x, 1).wait_send()
    a_many(x + 1, 1).wait_send()
    lax.fori_loop(0, x, drain, 0)
    finish(x)
    finish_last()
    drain(x, 0)
    copy1(final).wait_send()
    all4().wait_send()


def on_device(coils, pencils, kspace, sensitivity, line_index):
    _, coil_dev, part_dev, lines, nx = kspace.shape
    slab, ny, nz = sensitivity.shape[2:]
    chunks = slab // WIDE
    ring = coils // 4
    deep = ny // coils
    sizes = (pencils, coils, chunks, nx, ny, nz, lines)
    scale = 1.0 / math.sqrt(nx * ny * nz)
    rows = part_dev * lines
    wx = jnp.asarray(readout_table(nx, pencils))
    wy = jnp.asarray(phase_table(ny, lines, coils))
    wz = jnp.asarray(partition_table(nz, scale))
    block = (2, deep, nz)
    vmem = pltpu.VMEM
    dma = pltpu.SemaphoreType.DMA
    flat = kspace.reshape(2, coil_dev, rows, nx)
    return pl.pallas_call(
        functools.partial(kernel, sizes),
        out_shape=jax.ShapeDtypeStruct((2, slab, deep, nz), F32),
        in_specs=[
            pl.BlockSpec(memory_space=pl.ANY),
            pl.BlockSpec(memory_space=pl.ANY),
            pl.BlockSpec(memory_space=pl.ANY),
            pl.BlockSpec(memory_space=pl.ANY),
            pl.BlockSpec(memory_space=pl.ANY),
            pl.BlockSpec(memory_space=pl.ANY),
        ],
        out_specs=pl.BlockSpec(memory_space=pltpu.VMEM),
        scratch_shapes=[
            vmem(flat.shape, F32),
            vmem(sensitivity.shape, BF16),
            vmem(line_index.shape[::-1], jnp.int32),
            vmem(wx.shape, BF16),
            vmem(wy.shape, BF16),
            vmem(wz.shape, BF16),
            vmem((coil_dev, rows, 6 * nx), BF16),
            vmem((nz, 2 * lines), jnp.int32),
            vmem((slab, pencils * BLOCK, 128), F32),
            vmem((slab, pencils * BLOCK, 128), F32),
            vmem((WIDE, coil_dev * nz, 6 * ny), BF16),
            vmem((2 * ny, coil_dev * nz), F32),
            vmem((2 * ny, 6 * nz), BF16),
            vmem((slab, 2, ring, 2) + block, F32),
            vmem((slab, ring, 2) + block, F32),
            vmem((slab, ring - 1, 2) + block, F32),
            vmem((slab,) + block, F32),
            vmem((coils // 2 - 1,) + block, F32),
            dma((7,)),
        ]
        + [dma((slab,)) for _ in range(8)]
        + [dma((2,))],
        compiler_params=pltpu.CompilerParams(
            collective_id=0, has_side_effects=True, vmem_limit_bytes=62 * 1024 * 1024
        ),
    )(flat, sensitivity, line_index.T, wx, wy, wz)


def solution(mesh):
    in_specs = (P(None, "coil", "pencil", None, None), P(None, "coil", "pencil", None, None), P())
    out_specs = P(None, "pencil", "coil", None)
    return jax.shard_map(
        functools.partial(on_device, mesh.shape["coil"], mesh.shape["pencil"]),
        mesh=mesh,
        in_specs=in_specs,
        out_specs=out_specs,
        check_vma=False,
    )
```

```python
import functools
import math

import jax
import jax.numpy as jnp
import ml_dtypes
import numpy as np
from jax import lax
from jax.experimental import pallas as pl
from jax.experimental.pallas import tpu as pltpu
from jax.sharding import PartitionSpec as P

BF16 = jnp.bfloat16
F32 = jnp.float32
MESH = pl.DeviceIdType.MESH
WIDE = 2
RING_Y = 8
BLOCK = 8
NT = (((1,), (1,)), ((), ()))


def two_parts(values):
    high = values.astype(ml_dtypes.bfloat16)
    low = (values - high.astype(np.float64)).astype(ml_dtypes.bfloat16)
    return high, low


def wave(first, second, length):
    angle = (np.outer(first, second) % length) * (2.0 * math.pi / length)
    return np.cos(angle), np.sin(angle)


def readout_table(width, pencils):
    slab = width // pencils
    chunks = slab // WIDE
    cos, sin = wave(np.arange(width), np.arange(width), width)
    rows = np.stack([np.concatenate([cos, -sin], 1), np.concatenate([sin, cos], 1)])
    rows = rows.reshape(2, pencils, chunks, WIDE, 2 * width).transpose(2, 3, 0, 1, 4)
    high, low = two_parts(rows.reshape(chunks, 2 * WIDE * pencils, 2 * width))
    return np.concatenate([high, low, high], 2)


def phase_table(width, lines, slabs):
    group = width // lines
    freq = (np.arange(lines)[None, :] * group + np.arange(group)[:, None]).reshape(-1)
    cos, sin = wave(np.arange(width), freq, width)
    rows = np.stack([np.concatenate([cos, -sin], 1), np.concatenate([sin, cos], 1)])
    rows = rows.reshape(2, slabs // 2, 2, width // slabs, 2 * width).transpose(2, 0, 1, 3, 4)
    high, low = two_parts(rows.reshape(2, width, 2 * width))
    return np.concatenate([high, low, high], 2)


def partition_table(width, scale):
    freq = np.arange(width).reshape(width // 2, 2).transpose(1, 0).reshape(-1)
    cos, sin = wave(freq, np.arange(width), width)
    rows = np.concatenate([np.concatenate([cos, sin], 1), np.concatenate([-sin, cos], 1)], 0)
    high, low = two_parts(rows * scale)
    return np.concatenate([high, low, high], 0)


def kernel(
    sizes,
    kspace_hbm,
    sens_hbm,
    lines_hbm,
    wx_hbm,
    wy_hbm,
    wz_hbm,
    out_ref,
    kspace,
    sens,
    lines_ref,
    wx,
    wy,
    wz,
    parts,
    place,
    outbox,
    inbox,
    grid,
    planes,
    mixed,
    share,
    land1,
    land2,
    land3,
    land4,
    load_sem,
    a_send,
    a_recv,
    s1,
    r1,
    s2,
    r2,
    s3,
    r3,
    s4,
):
    pencils, coils, chunks, nx, ny, nz, lines = sizes
    ring = coils // 4
    deep = ny // coils
    coil = lax.axis_index("coil")
    me = lax.axis_index("pencil")
    core = coil % 2
    hi = coil // 2 % 2
    col = coil // 4
    other_core = coil + 1 - 2 * core
    other_hi = coil + 2 - 4 * hi

    pairs = [
        (kspace_hbm, kspace),
        (wx_hbm.at[0], wx.at[0]),
        (wx_hbm.at[pl.ds(1, chunks - 1)], wx.at[pl.ds(1, chunks - 1)]),
        (lines_hbm, lines_ref),
        (wy_hbm, wy),
        (wz_hbm, wz),
        (sens_hbm, sens),
    ]
    loads = [
        pltpu.make_async_copy(src, dst, load_sem.at[i]) for i, (src, dst) in enumerate(pairs)
    ]
    for load in loads[:2]:
        load.start()

    barrier = pltpu.get_barrier_semaphore()

    def greet(to_coil, to_pencil):
        pl.semaphore_signal(
            barrier, inc=1, device_id=(to_coil, to_pencil), device_id_type=MESH
        )

    def greet_pencil(d, carry):
        greet(coil, (me + d) % pencils)
        return carry

    lax.fori_loop(1, pencils, greet_pencil, 0)
    greet(other_core, me)
    for d in range(1, coils // 2):
        greet((coil + 2 * d) % coils, me)

    loads[0].wait()
    for load in loads[2:]:
        load.start()
    for c in range(2):
        for comp in range(2):
            value = kspace[comp, c]
            high = value.astype(BF16)
            low = (value - high.astype(F32)).astype(BF16)
            parts[c, :, pl.ds(comp * nx, nx)] = high
            parts[c, :, pl.ds((2 + comp) * nx, nx)] = high
            parts[c, :, pl.ds((4 + comp) * nx, nx)] = low
    loads[1].wait()

    def readout(j):
        for c in range(2):
            result = lax.dot_general(wx[j], parts[c], NT, preferred_element_type=F32)
            for x in range(WIDE):
                for comp in range(2):
                    rows = (x * 2 + comp) * pencils
                    for zp in range(2):
                        to = pl.ds(zp * 4 + c * 2 + comp, pencils, stride=BLOCK)
                        outbox[j * WIDE + x, to, :] = result[
                            rows : rows + pencils, zp * 128 : (zp + 1) * 128
                        ]

    def at(pencil):
        return pl.ds(pl.multiple_of(pencil * BLOCK, BLOCK), BLOCK)

    def a_copy(x, count, to):
        return pltpu.make_async_remote_copy(
            src_ref=outbox.at[pl.ds(x, count), at(to), :],
            dst_ref=inbox.at[pl.ds(x, count), at(me), :],
            send_sem=a_send.at[x],
            recv_sem=a_recv.at[x],
            device_id=(coil, to),
            device_id_type=MESH,
        )

    def a_many(x, count):
        return pltpu.make_async_remote_copy(
            src_ref=outbox.at[pl.ds(x, count), pl.ds(0, (pencils - 1) * BLOCK), :],
            dst_ref=inbox.at[pl.ds(x, count), pl.ds(0, (pencils - 1) * BLOCK), :],
            send_sem=a_send.at[x],
            recv_sem=a_recv.at[x],
            device_id=(coil, me),
            device_id_type=MESH,
        )

    def send(x, count):
        def one(i, carry):
            k, g = i // RING_Y, i % RING_Y
            dy = 1 + g // 4 + 4 * (g % 2) + 2 * (g % 4 // 2)
            dz = k + g + 2
            to = (me // RING_Y + dz) % (pencils // RING_Y) * RING_Y + (me + dy) % RING_Y
            a_copy(x, count, to).start()
            return carry

        lax.fori_loop(0, pencils - 1, one, 0)
        for k in range(count):
            inbox[x + k, at(me), :] = outbox[x + k, at(me), :]

    half = lax.broadcasted_iota(jnp.int32, (nz // 2, 128), 1) // 64

    def fill(x, buf):
        for zl in range(2):
            spot = place[pl.ds(zl, nz // 2, stride=2), :]
            keep01 = spot == half
            keep23 = spot == half + 2
            for c in range(2):
                for comp in range(2):
                    value = inbox[x, pl.ds(c * 2 + comp, nz // 2, stride=4), :]
                    turned = pltpu.roll(value, 64, 1)
                    if zl == 0:
                        both = jnp.where(half == 0, value, turned)
                    else:
                        both = jnp.where(half == 0, turned, value)
                    for k, keep in enumerate((keep01, keep23)):
                        kept = jnp.where(keep, both, 0.0)
                        high = kept.astype(BF16)
                        low = (kept - high.astype(F32)).astype(BF16)
                        rows = pl.ds(c * nz + zl * (nz // 2), nz // 2)
                        left = comp * ny + k * 128
                        grid[buf, rows, pl.ds(left, 128)] = high
                        grid[buf, rows, pl.ds(2 * ny + left, 128)] = high
                        grid[buf, rows, pl.ds(4 * ny + left, 128)] = low

    def transform(buf, part, count):
        tall = ny // 2
        top = part if count == 1 else 0
        table = wy[pl.ds(top, count)].reshape(count * ny, 6 * ny)
        planes[pl.ds(0, count * ny), :] = lax.dot_general(
            table, grid[buf], NT, preferred_element_type=F32
        )
        for p in range(count):
            for c in range(2):
                for comp in range(2):
                    value = planes[pl.ds(p * ny + comp * tall, tall), pl.ds(c * nz, nz)]
                    high = value.astype(BF16)
                    low = (value - high.astype(F32)).astype(BF16)
                    rows = pl.ds(p * ny + c * tall, tall)
                    mixed[rows, pl.ds(comp * nz, nz)] = high
                    mixed[rows, pl.ds((2 + comp) * nz, nz)] = high
                    mixed[rows, pl.ds((4 + comp) * nz, nz)] = low
        return jnp.dot(mixed[pl.ds(0, count * ny), :], wz[...], preferred_element_type=F32)

    def combine(x, buf, part, count):
        image = transform(buf, part, count)
        for p in range(count):
            home = part if count == 1 else p
            for m in range(coils // 2):
                real_part = 0.0
                imag_part = 0.0
                for c in range(2):
                    top = p * ny + c * (ny // 2) + m * deep
                    re = image[top : top + deep, :nz]
                    im = image[top : top + deep, nz:]
                    first = (2 * m + home) * deep
                    if count == 1:
                        first = pl.multiple_of(first, deep)
                    sre = sens[0, c, x, pl.ds(first, deep), :].astype(F32)
                    sim = sens[1, c, x, pl.ds(first, deep), :].astype(F32)
                    real_part = real_part + sre * re + sim * im
                    imag_part = imag_part + sre * im - sim * re
                share[x, home, m // 2, m % 2, 0] = real_part
                share[x, home, m // 2, m % 2, 1] = imag_part

    def compute(x, buf):
        fill(x, buf)
        combine(x, buf, 0, 2)
        copy1(x).start()

    def compute_halves(x, buf):
        fill(x, buf)
        combine(x, buf, 1 - core, 1)
        copy1(x).start()
        combine(x, buf, core, 1)

    def copy1(j):
        return pltpu.make_async_remote_copy(
            src_ref=share.at[j, 1 - core],
            dst_ref=land1.at[j],
            send_sem=s1.at[j],
            recv_sem=r1.at[j],
            device_id=(other_core, me),
            device_id_type=MESH,
        )

    def copy2(j, d):
        return pltpu.make_async_remote_copy(
            src_ref=share.at[j, core, (col + d) % ring],
            dst_ref=land2.at[j, d - 1],
            send_sem=s2.at[j],
            recv_sem=r2.at[j],
            device_id=((coil + 4 * d) % coils, me),
            device_id_type=MESH,
        )

    def all2(j):
        return pltpu.make_async_remote_copy(
            src_ref=land2.at[j],
            dst_ref=land2.at[j],
            send_sem=s2.at[j],
            recv_sem=r2.at[j],
            device_id=((coil + 4) % coils, me),
            device_id_type=MESH,
        )

    def copy3(j):
        return pltpu.make_async_remote_copy(
            src_ref=share.at[j, core, col, 1 - hi],
            dst_ref=land3.at[j],
            send_sem=s3.at[j],
            recv_sem=r3.at[j],
            device_id=(other_hi, me),
            device_id_type=MESH,
        )

    def straight(d):
        to = (coil + 2 * d) % coils
        return pltpu.make_async_remote_copy(
            src_ref=share.at[final, core, to // 4, to // 2 % 2],
            dst_ref=land4.at[d - 1],
            send_sem=s4.at[0],
            recv_sem=s4.at[1],
            device_id=(to, me),
            device_id_type=MESH,
        )

    def all4():
        return pltpu.make_async_remote_copy(
            src_ref=land4,
            dst_ref=land4,
            send_sem=s4.at[0],
            recv_sem=s4.at[1],
            device_id=(other_hi, me),
            device_id_type=MESH,
        )

    def step2(x):
        copy1(x).wait_recv()
        share[x, core] = share[x, core] + land1[x]

        def usual():
            for d in range(1, ring):
                copy2(x, d).start()

        def direct():
            for d in range(1, coils // 2):
                straight(d).start()

        if isinstance(x, int) and x == final:
            direct()
        else:
            usual()

    def sum3(x):
        all2(x).wait_recv()
        total = share[x, core, col]
        for d in range(ring - 1):
            total = total + land2[x, d]
        share[x, core, col] = total

    def send3(x):
        copy3(x).start()

    def finish(x):
        copy3(x).wait_recv()
        total = share[x, core, col, hi] + land3[x]
        for comp in range(2):
            out_ref[comp, x] = total[comp]

    def finish_last():
        all4().wait_recv()
        total = share[final, core, col, hi]
        for d in range(coils // 2 - 1):
            total = total + land4[d]
        for comp in range(2):
            out_ref[comp, final] = total[comp]

    last = chunks - 1
    final = chunks * WIDE - 1

    def early(j):
        readout(j)

        @pl.when(j < last)
        def _():
            send(j * WIDE, 2)

        @pl.when(j == last)
        def _():
            send(j * WIDE, 1)
            send(j * WIDE + 1, 1)

    readout(0)
    pl.semaphore_wait(barrier, pencils - 1 + coils // 2)
    send(0, 2)
    loads[2].wait()
    readout(1)
    send(2, 2)
    loads[3].wait()
    here = lines_ref[...] - (ny // lines) * lax.broadcasted_iota(jnp.int32, (lines, nz), 0)
    place[...] = jnp.concatenate([here, here], 0).T

    for load in loads[4:]:
        load.wait()

    def turn(j, carry):
        x = j * WIDE

        @pl.when(j + 2 <= last)
        def _():
            early(j + 2)

        a_many(x, 2).wait_recv()
        fill(x, 0)
        fill(x + 1, 1)
        combine(x, 0, 0, 2)
        copy1(x).start()

        @pl.when(j >= 1)
        def _():
            step2(x - 1)

        combine(x + 1, 1, 0, 2)
        copy1(x + 1).start()
        step2(x)

        @pl.when(j >= 2)
        def _():
            sum3(x - 3)
            send3(x - 3)

        @pl.when(j >= 1)
        def _():
            sum3(x - 2)
            send3(x - 2)

        return carry

    lax.fori_loop(0, last, turn, 0)
    x = last * WIDE
    a_many(x, 1).wait_recv()
    compute(x, 0)
    step2(x - 1)
    for k in (3, 2):
        sum3(x - k)
        send3(x - k)
    a_many(x + 1, 1).wait_recv()
    step2(x)
    compute_halves(final, 1)
    sum3(x - 1)
    send3(x - 1)
    step2(final)
    for k in range(x - 3):
        finish(k)
    sum3(x)
    send3(x)
    for k in range(x - 3, x):
        finish(k)

    def drain(j, carry):
        copy1(j).wait_send()
        all2(j).wait_send()
        copy3(j).wait_send()
        return carry

    for j in range(last):
        a_many(j * WIDE, 2).wait_send()
    a_many(x, 1).wait_send()
    a_many(x + 1, 1).wait_send()
    lax.fori_loop(0, x, drain, 0)
    finish(x)
    finish_last()
    drain(x, 0)
    copy1(final).wait_send()
    all4().wait_send()


def on_device(coils, pencils, kspace, sensitivity, line_index):
    _, coil_dev, part_dev, lines, nx = kspace.shape
    slab, ny, nz = sensitivity.shape[2:]
    chunks = slab // WIDE
    ring = coils // 4
    deep = ny // coils
    sizes = (pencils, coils, chunks, nx, ny, nz, lines)
    scale = 1.0 / math.sqrt(nx * ny * nz)
    rows = part_dev * lines
    wx = jnp.asarray(readout_table(nx, pencils))
    wy = jnp.asarray(phase_table(ny, lines, coils))
    wz = jnp.asarray(partition_table(nz, scale))
    block = (2, deep, nz)
    vmem = pltpu.VMEM
    dma = pltpu.SemaphoreType.DMA
    flat = kspace.reshape(2, coil_dev, rows, nx)
    return pl.pallas_call(
        functools.partial(kernel, sizes),
        out_shape=vmem((2, slab, deep, nz), F32),
        in_specs=[
            pl.BlockSpec(memory_space=pl.ANY),
            pl.BlockSpec(memory_space=pl.ANY),
            pl.BlockSpec(memory_space=pl.ANY),
            pl.BlockSpec(memory_space=pl.ANY),
            pl.BlockSpec(memory_space=pl.ANY),
            pl.BlockSpec(memory_space=pl.ANY),
        ],
        out_specs=pl.BlockSpec(memory_space=pltpu.VMEM),
        scratch_shapes=[
            vmem(flat.shape, F32),
            vmem(sensitivity.shape, BF16),
            vmem(line_index.shape[::-1], jnp.int32),
            vmem(wx.shape, BF16),
            vmem(wy.shape, BF16),
            vmem(wz.shape, BF16),
            vmem((coil_dev, rows, 6 * nx), BF16),
            vmem((nz, 2 * lines), jnp.int32),
            vmem((slab, pencils * BLOCK, 128), F32),
            vmem((slab, pencils * BLOCK, 128), F32),
            vmem((WIDE, coil_dev * nz, 6 * ny), BF16),
            vmem((2 * ny, coil_dev * nz), F32),
            vmem((2 * ny, 6 * nz), BF16),
            vmem((slab, 2, ring, 2) + block, F32),
            vmem((slab, ring, 2) + block, F32),
            vmem((slab, ring - 1, 2) + block, F32),
            vmem((slab,) + block, F32),
            vmem((coils // 2 - 1,) + block, F32),
            dma((7,)),
        ]
        + [dma((slab,)) for _ in range(8)]
        + [dma((2,))],
        compiler_params=pltpu.CompilerParams(
            collective_id=0, has_side_effects=True, vmem_limit_bytes=62 * 1024 * 1024
        ),
    )(flat, sensitivity, line_index.T, wx, wy, wz)


def solution(mesh):
    in_specs = (P(None, "coil", "pencil", None, None), P(None, "coil", "pencil", None, None), P())
    out_specs = P(None, "pencil", "coil", None)
    return jax.shard_map(
        functools.partial(on_device, mesh.shape["coil"], mesh.shape["pencil"]),
        mesh=mesh,
        in_specs=in_specs,
        out_specs=out_specs,
        check_vma=False,
    )
```
